32 devices in a mesh: row: 4 (over y, x), col: 8 (over z, core).
Axes of the slice: x: 2, y: 2, z: 4, core: 2. Of those that a mesh axis runs over, the one named last changes fastest.
Arguments:
- corner: float32 [18432, 18432], P('row', 'col'), may hold values from -0.046875 to 0.046875
- right_proj: float32 [18432, 512], P('col', 'row'), may hold values from -1.5 to 1.5
- left_proj: float32 [18432, 512], P('row', 'col'), may hold values from -1.5 to 1.5
- upstream: float32 [512, 512], replicated, may hold values from -0.25 to 0.25
Outputs:
- corner_right: float32 [18432, 512], P(('row', 'col'))
- corner_left: float32 [18432, 512], P(('col', 'row'))
- right_grad: float32 [18432, 512], P(('col', 'row'))
- left_grad: float32 [18432, 512], P(('row', 'col'))
- corner_grad: float32 [18432, 18432], P('row', 'col')
The draws below stay inside these ranges and needn't reach their ends.
All inputs are finite; a program needn't handle non-finite values.
Results may differ from the reference program's by a relative error of at most 0.00007.
Values sent between devices are 32-bit elements; how exact they have to be, the bound alone decides.
A program may use at most 192 MiB of HBM per device.

```python
import jax
import jax.numpy as jnp
from jax import lax

ORDER = 18432
CHI = 512


def shard_levels(stream_key, dims, cuts, smallest, high):
    loudness, own = 1.0, jax.random.fold_in(stream_key, 6)
    for axis_at, parts in cuts:
        draws = jnp.exp(jax.random.uniform(jax.random.fold_in(own, axis_at), (parts,), jnp.float32, smallest / len(cuts), high / len(cuts)))
        loudness = loudness * jnp.repeat(draws, dims[axis_at] // parts).reshape([-1 if axis == axis_at else 1 for axis in range(len(dims))])
    return loudness


def gaussian(key, extent, scale, bound, cuts=(), dtype=jnp.bfloat16):
    entries = jax.random.normal(key, extent, jnp.float32) * scale
    if len(cuts) > 0:
        entries = shard_levels(key, extent, cuts, -0.22, 0.18) * entries
    return jnp.clip(entries, min=-bound, max=bound).astype(dtype)


def setup_inputs(seed: int = 0) -> dict:
    arg_keys = jax.random.split(jax.random.key(seed), 5)
    corner = gaussian(arg_keys[0], (ORDER, ORDER), ORDER ** -0.5, 0.046875, ((0, 4), (1, 8)), jnp.float32)
    right_proj = gaussian(arg_keys[1], (ORDER, CHI), 0.25, 1.5, ((0, 8), (1, 4)), jnp.float32)
    left_proj = gaussian(arg_keys[2], (ORDER, CHI), 0.25, 1.5, ((0, 4), (1, 8)), jnp.float32)
    upstream = gaussian(arg_keys[3], (CHI, CHI), CHI ** -0.5, 0.25, (), jnp.float32)
    return {"corner": corner, "right_proj": right_proj, "left_proj": left_proj, "upstream": upstream}


def reference(corner, right_proj, left_proj, upstream):
    best = lax.Precision.HIGHEST
    corner_right = jnp.dot(corner, right_proj, precision=best, preferred_element_type=jnp.float32)
    corner_left = jnp.dot(corner.T, left_proj, precision=best, preferred_element_type=jnp.float32)
    weighted = jnp.dot(left_proj, upstream, precision=best, preferred_element_type=jnp.float32)
    corner_grad = jnp.dot(weighted, right_proj.T, precision=best, preferred_element_type=jnp.float32)
    right_grad = jnp.dot(corner_left, upstream, precision=best, preferred_element_type=jnp.float32)
    left_grad = jnp.dot(corner_right, upstream.T, precision=best, preferred_element_type=jnp.float32)
    return corner_right, corner_left, right_grad, left_grad, corner_grad
```

```python
import functools

import jax
import jax.numpy as jnp
from jax import lax
from jax.experimental import pallas as pl
from jax.experimental.pallas import tpu as pltpu
from jax.sharding import PartitionSpec as P

VMEM = 60 * 1024 * 1024


def split(x):
    high = x.astype(jnp.bfloat16)
    return high, (x - high.astype(jnp.float32)).astype(jnp.bfloat16)


def product(a, b):
    dot = functools.partial(jnp.dot, preferred_element_type=jnp.float32)
    return dot(a[0], b[0]) + (dot(a[0], b[1]) + dot(a[1], b[0]))


def block_of(size, limit, unit):
    fits = [n for n in range(unit, limit + 1, unit) if size % n == 0]
    return fits[-1] if fits else size


def call(kernel, grid, ins, out_spec, out_shape, scratch, flops, moved):
    return pl.pallas_call(
        kernel,
        grid=grid,
        in_specs=ins,
        out_specs=out_spec,
        out_shape=jax.ShapeDtypeStruct(out_shape, jnp.float32),
        scratch_shapes=scratch,
        compiler_params=pltpu.CompilerParams(vmem_limit_bytes=VMEM),
        cost_estimate=pl.CostEstimate(flops=flops, bytes_accessed=moved, transcendentals=0),
    )


def whole(shape):
    return pl.BlockSpec(shape, lambda i: (0, 0), pipeline_mode=pl.Buffered(1))


def right_kernel(corner_ref, proj_ref, out_ref, high, low):
    @pl.when(pl.program_id(0) == 0)
    def _():
        high[...], low[...] = split(proj_ref[...])

    out_ref[...] = product(split(corner_ref[...]), (high[...], low[...]))


def right_product(corner, proj, parts, chunk, chunks):
    rows, depth = corner.shape
    chi = proj.shape[1]
    tile = rows // parts // chunks
    return call(
        right_kernel,
        (parts,),
        [pl.BlockSpec((tile, depth), lambda i: (i * chunks + chunk, 0)), whole((depth, chi))],
        pl.BlockSpec((tile, chi), lambda i: (i, 0)),
        (rows // chunks, chi),
        [pltpu.VMEM((depth, chi), jnp.bfloat16)] * 2,
        6 * rows * depth * chi // chunks,
        4 * rows * depth // chunks,
    )(corner, proj)


def left_kernel(corner_ref, proj_ref, out_ref, high, low):
    @pl.when(pl.program_id(0) == 0)
    def _():
        high[...], low[...] = split(proj_ref[...])

    out_ref[...] = product((high[...], low[...]), split(corner_ref[...])).T


def left_product(corner, proj_t):
    rows, width = corner.shape
    chi = proj_t.shape[0]
    tile = block_of(width, 256, 128)
    return call(
        left_kernel,
        (width // tile,),
        [pl.BlockSpec((rows, tile), lambda i: (0, i)), whole((chi, rows))],
        pl.BlockSpec((tile, chi), lambda i: (i, 0)),
        (width, chi),
        [pltpu.VMEM((chi, rows), jnp.bfloat16)] * 2,
        6 * rows * width * chi,
        4 * rows * width,
    )(corner, proj_t)


def grad_kernel(left_ref, up_ref, right_ref, out_ref, high, low):
    @pl.when(pl.program_id(0) == 0)
    def _():
        high[...], low[...] = split(product(split(up_ref[...]), split(right_ref[...].T)))

    out_ref[...] = product(split(left_ref[...].T), (high[...], low[...]))


def grad_product(proj_t, upstream, right):
    chi, rows = proj_t.shape
    width = right.shape[0]
    tile = block_of(rows, 512, 128)
    return call(
        grad_kernel,
        (rows // tile,),
        [pl.BlockSpec((chi, tile), lambda i: (0, i)), whole((chi, chi)), whole((width, chi))],
        pl.BlockSpec((tile, width), lambda i: (i, 0)),
        (rows, width),
        [pltpu.VMEM((chi, width), jnp.bfloat16)] * 2,
        6 * rows * width * chi,
        4 * rows * width,
    )(proj_t, upstream, right)


def swaps(name, n):
    me = lax.axis_index(name)
    for step in range(1, n):
        if n & (n - 1):
            yield [(i, (i + step) % n) for i in range(n)], (me + step) % n, (me - step + n) % n
        else:
            yield [(i, i ^ step) for i in range(n)], me ^ step, me ^ step


def gather(x, name, n, axis):
    size = x.shape[axis]
    shape = list(x.shape)
    shape[axis] = n * size
    got = [(lax.axis_index(name), x)]
    got += [(source, lax.ppermute(x, name, pairs)) for pairs, _, source in swaps(name, n)]
    out = jnp.zeros(shape, x.dtype)
    for owner, block in got:
        out = lax.dynamic_update_slice_in_dim(out, block, owner * size, axis)
    return out


def scatter_sum(x, name, n):
    size = x.shape[0] // n
    mine = functools.partial(lax.dynamic_slice_in_dim, x, slice_size=size, axis=0)
    total = mine(lax.axis_index(name) * size)
    for pairs, target, _ in swaps(name, n):
        total += lax.ppermute(mine(target * size), name, pairs)
    return total


def body(rows, parts, corner, right_proj, left_proj, upstream):
    high = lax.Precision.HIGH
    chunks = 1
    right = gather(right_proj, "row", rows, 1)
    left_t = lax.all_gather(left_proj.T, "col", axis=0, tiled=True)
    pieces = [right_product(corner, right, parts, c, chunks) for c in range(chunks)]
    pieces, left_t = lax.optimization_barrier((pieces, left_t))
    pieces = [lax.psum_scatter(p, "col", scatter_dimension=0, tiled=True) for p in pieces]
    partial_left = left_product(corner, left_t)
    corner_left = scatter_sum(partial_left, "row", rows)
    corner_grad = grad_product(left_t, upstream, right)
    corner_right = jnp.concatenate(pieces, axis=0)
    right_grad = jnp.dot(corner_left, upstream, precision=high, preferred_element_type=jnp.float32)
    left_grad = lax.dot_general(
        corner_right, upstream, (((1,), (1,)), ((), ())), precision=high, preferred_element_type=jnp.float32
    )
    return (corner_right, corner_left, right_grad, left_grad, corner_grad)


def solution(mesh):
    return jax.shard_map(
        functools.partial(body, mesh.shape["row"], mesh.shape["col"]),
        mesh=mesh,
        in_specs=(P("row", "col"), P("col", "row"), P("row", "col"), P()),
        out_specs=(
            P(("row", "col"), None),
            P(("col", "row"), None),
            P(("col", "row"), None),
            P(("row", "col"), None),
            P("row", "col"),
        ),
        check_vma=False,
    )
```
